128 devices in a mesh: occ: 8 (over z, core), vir: 16 (over x, y).
Axes of the slice: x: 4, y: 4, z: 4, core: 2. Of those that a mesh axis runs over, the one named last changes fastest.
Arguments:
- amplitudes: bfloat16 [640, 8, 640], P('vir', 'occ'), may hold values from -6 to 6
- tile_list: int32 [8, 5, 1], replicated, may hold values from 0 to 4, as said below
- ladder_factor: bfloat16 [1280, 640, 640], P(('occ', 'vir')), may hold values from -0.0625 to 0.0625
- fock_vv: bfloat16 [640, 640], replicated, may hold values from -0.25 to 0.25
- pair_coupling: float32 [8, 8], replicated, may hold values from -2 to 2
Outputs:
- residual: float32 [640, 8, 640], P('vir', 'occ')
The draws below stay inside these ranges and needn't reach their ends.
Inputs may be any that keep to these rules, and one draw needn't show every extreme that they name: For each pair p and tile t of a, tile_list[p, t, 0] names the single tile of b that is present.
All inputs are finite; a program needn't handle non-finite values.
Results may differ from the reference program's by a relative error of at most 0.0023.
Values may be sent and summed in bfloat16 or wider, within the bound.
No kernel may reach another device: no remote copies, remote signals or barrier semaphores. Data moves between devices by JAX's collectives and lax.ppermute only.
A program may use at most 128 MiB of HBM per device.

```python
import jax
import jax.numpy as jnp
from jax import lax

V = 640
VT = 128
KT = 1
L = 1280
NT = 5
PAIRS = 8


def draw_tile_list(key, part):
    key = jax.random.fold_in(key, 11)
    keys = jax.random.split(key, PAIRS * NT)

    def order_one(single):
        return jax.random.permutation(single, NT)
    orders = jax.vmap(order_one)(keys)
    chosen = jnp.sort(orders[:, :KT], axis=1)
    return chosen.reshape(PAIRS, NT, KT).astype(jnp.int32)


def steps_of(rng, shape, cuts, least, high):
    factor_of = 1.0
    for position, shards_of in cuts:
        steps = jax.random.uniform(jax.random.fold_in(jax.random.fold_in(rng, 6), position), (shards_of,), jnp.float32, least / len(cuts), high / len(cuts))
        factor_of = factor_of * jnp.repeat(jnp.exp(steps), shape[position] // shards_of).reshape((-1,) + (1,) * (len(shape) - 1 - position))
    return factor_of


def centred(key, extent, scale, reach, shards=(), held_as=jnp.bfloat16):
    entries = scale * jax.random.normal(key, extent, jnp.float32)
    if shards:
        entries = entries * steps_of(key, extent, shards, -0.22, 0.18)
    return jnp.clip(entries, -reach, reach).astype(held_as)


def setup_inputs(seed: int = 0) -> dict:
    arg_keys = jax.random.split(jax.random.key(seed), 6)
    amplitudes = centred(arg_keys[0], (V, PAIRS, V), 1.0, 6.0, ((0, 16), (1, 8)))
    tile_list = draw_tile_list(jax.random.fold_in(arg_keys[5], 71), 0)
    ladder_factor = centred(arg_keys[2], (L, V, V), (V * 16) ** -0.5, 0.0625, ((0, 128),))
    fock_vv = centred(arg_keys[3], (V, V), V ** -0.5, 0.25)
    pair_coupling = centred(arg_keys[4], (PAIRS, PAIRS), PAIRS ** -0.5, 2.0, (), jnp.float32)
    return dict(amplitudes=amplitudes, tile_list=tile_list, ladder_factor=ladder_factor, fock_vv=fock_vv, pair_coupling=pair_coupling)


def expand_rows(compact, row_lists):
    blocks = []
    for tile_b in range(NT):
        block = jnp.zeros(compact.shape[:-1] + (VT,), jnp.float32)
        for slot in range(row_lists.shape[-1]):
            chosen = (row_lists[..., slot] == tile_b)[..., None]
            block = block + jnp.where(chosen, compact[..., slot * VT:(slot + 1) * VT], jnp.zeros_like(block))
        blocks.append(block)
    return jnp.concatenate(blocks, axis=-1)


def pair_block(amps_wide, lists, factor_wide):
    depth = factor_wide.shape[0]
    halves = []
    for tile_c in range(NT):
        running_total = jnp.zeros((depth, VT, V), jnp.float32)
        for slot in range(lists.shape[1]):
            start = (lists[tile_c, slot] * VT).astype(jnp.int32)
            amplitude_tile = lax.dynamic_slice(amps_wide, (jnp.int32(tile_c * VT), start), (VT, VT))
            integral_panel = lax.dynamic_slice_in_dim(factor_wide, start, VT, 2)
            running_total = running_total + jnp.einsum("aw,vyw->vay", amplitude_tile, integral_panel)
        rounded = lax.optimization_barrier(running_total.astype(jnp.bfloat16))
        halves.append(rounded.astype(jnp.float32))
    half = jnp.concatenate(halves, axis=1)
    rows_out = []
    for tile_a in range(NT):
        brow = factor_wide[:, tile_a * VT:(tile_a + 1) * VT, :]
        pieces = []
        for slot in range(lists.shape[1]):
            start = (lists[tile_a, slot] * VT).astype(jnp.int32)
            yslab = lax.dynamic_slice_in_dim(half, start, VT, 2)
            pieces.append(jnp.einsum("lrc,lcs->rs", brow, yslab))
        rows_out.append(jnp.concatenate(pieces, axis=1))
    return jnp.concatenate(rows_out, axis=0)


def reference(amplitudes, tile_list, ladder_factor, fock_vv, pair_coupling):
    row_lists = jnp.repeat(tile_list, VT, axis=1)
    tiles = jnp.arange(V, dtype=jnp.int32) // VT
    kept_pv = jnp.any(row_lists[:, :, :, None] == tiles, axis=2)
    kept_mask = jnp.transpose(kept_pv, (1, 0, 2))
    masked = jnp.where(kept_mask, amplitudes, jnp.zeros_like(amplitudes))
    pair_major = jnp.transpose(masked, (1, 0, 2))
    factor_blocks = ladder_factor.reshape(L // 16, 16, V, V)
    slots = tile_list.shape[2]

    def one_pair(inputs):
        pair_amps, lists = inputs
        amps_wide = pair_amps.astype(jnp.float32)

        def step_block(running, factor_block):
            return running + pair_block(amps_wide, lists, factor_block.astype(jnp.float32)), None

        running, unused = lax.scan(step_block, jnp.zeros((V, slots * VT), jnp.float32), factor_blocks)
        return running

    compact = lax.map(one_pair, (pair_major, tile_list))
    ladder = jnp.transpose(expand_rows(compact, row_lists), (1, 0, 2))
    masked_broad_panel = masked.astype(jnp.float32)
    broad_fock_matrix = fock_vv.astype(jnp.float32)
    hole_term = jnp.einsum("aqb,qp->apb", masked_broad_panel, pair_coupling, precision=lax.Precision.HIGHEST)
    virtual_fock_part = jnp.einsum("gr,rvo->gvo", broad_fock_matrix, masked_broad_panel) + jnp.einsum("wlu,nu->wln", masked_broad_panel, broad_fock_matrix)
    combined = ladder + hole_term + virtual_fock_part
    return jnp.where(kept_mask, combined, jnp.zeros_like(combined))
```

```python
import jax
import jax.numpy as jnp
from jax import lax
from jax.experimental import pallas as pl
from jax.experimental.pallas import tpu as pltpu
from jax.sharding import Mesh
from jax.sharding import PartitionSpec as P

F32 = jnp.float32
BF16 = jnp.bfloat16
NT = (((1,), (1,)), ((), ()))
TILE = 128
SAME_CORE = ("z", "x", "y")
VMEM_LIMIT = 60 << 20


def row_tiles(lists, pair, vir, rows):
    first = vir * rows
    low = first // TILE
    high = (first + rows - 1) // TILE
    index = lax.broadcasted_iota(jnp.int32, (rows, TILE), 0) + first
    return low, high, index < (low + 1) * TILE


def compact_kernel(place, lists, amps, out):
    pair, vir = place[0], place[1]
    rows, width = amps.shape
    low, high, in_low = row_tiles(lists, pair, vir, rows)
    chosen = jnp.where(in_low, lists[pair, low], lists[pair, high])
    kept = jnp.zeros((rows, TILE), F32)
    for tile in range(width // TILE):
        part = amps[:, tile * TILE : (tile + 1) * TILE].astype(F32)
        kept = jnp.where(chosen == tile, part, kept)
    out[...] = jnp.broadcast_to(kept.astype(BF16)[None], out.shape)


def ladder_kernel(place, lists, amps, own, other, out, factor, half, items, sems):
    core = place[2]
    pairs, tiles = amps.shape[0], lists.shape[1]
    depth = own.shape[0]
    width = tiles * TILE
    copies = [
        pltpu.make_async_copy(src, factor.at[chunk], sems.at[chunk])
        for chunk, src in enumerate((own, other))
    ]
    for copy in copies:
        copy.start()
    count = jnp.int32(0)
    for pair in range(pairs):
        for tile in range(tiles):
            need = lists[2 * pair + core, 0] == tile
            for row in range(1, tiles):
                need = need | (lists[2 * pair + core, row] == tile)
            items[count] = jnp.int32(pair * 8 + tile)
            count = count + need.astype(jnp.int32)
    items[count] = items[count - 1]

    def half_of(chunk, index):
        item = items[index]
        pair, tile = item // 8, item % 8
        b_rows = pl.ds(pl.multiple_of(tile * TILE, TILE), TILE)
        for tile_c in range(tiles):
            start = pl.multiple_of(lists[2 * pair + core, tile_c] * TILE, TILE)
            panel = factor[chunk, :, b_rows, pl.ds(start, TILE)].reshape(depth * TILE, TILE)
            rows = amps[pair, tile_c * TILE : (tile_c + 1) * TILE, :]
            result = lax.dot_general(rows, panel, NT, preferred_element_type=F32).astype(BF16)
            for level in range(depth):
                first = level * width + tile_c * TILE
                half[pair * tiles + tile, first : first + TILE, :] = result[:, level * TILE : (level + 1) * TILE]

    for chunk in range(2):
        copies[chunk].wait()

        def two_items(step, carry):
            half_of(chunk, 2 * step)
            half_of(chunk, 2 * step + 1)
            return carry

        lax.fori_loop(0, (count + 1) // 2, two_items, 0)

        def tile_row(tile_a, carry):
            a_rows = pl.ds(pl.multiple_of(tile_a * TILE, TILE), TILE)
            left = jnp.concatenate([factor[chunk, level, a_rows, :] for level in range(depth)], axis=1)
            right = jnp.concatenate(
                [half[pair * tiles + lists[2 * pair + core, tile_a]] for pair in range(pairs)], axis=1
            )
            result = jnp.dot(left, right, preferred_element_type=F32)
            for pair in range(pairs):
                value = result[:, pair * TILE : (pair + 1) * TILE]
                if chunk == 0:
                    out[pair, a_rows, :] = value
                else:
                    out[pair, a_rows, :] += value
            return carry

        lax.fori_loop(0, tiles, tile_row, 0)


def local_kernel(place, lists, coupling, own_side, other_side, amps, fock_rows, fock, out):
    pair, vir, core = place[0], place[1], place[2]
    pairs, rows = own_side.shape[0], own_side.shape[1]
    tiles = lists.shape[1]
    low, high, in_low = row_tiles(lists, pair, vir, rows)
    tile_low, tile_high = lists[pair, low], lists[pair, high]
    total = jnp.zeros((rows, TILE), F32)
    for side, held in ((core, own_side), (1 - core, other_side)):
        for index in range(pairs):
            other = 2 * index + side
            weight = coupling[other, pair]
            none = jnp.float32(0)
            weight_low = jnp.where(lists[other, low] == tile_low, weight, none)
            weight_high = jnp.where(lists[other, high] == tile_high, weight, none)
            total = total + held[index].astype(F32) * jnp.where(in_low, weight_low, weight_high)
    chosen = jnp.where(in_low, tile_low, tile_high)
    masked = []
    for tile_c in range(tiles):
        part = fock_rows[vir, :, tile_c * TILE : (tile_c + 1) * TILE].astype(F32)
        masked.append(jnp.where(chosen == lists[pair, tile_c], part, jnp.zeros_like(part)).astype(BF16))
    left = jnp.concatenate(masked, axis=1)
    total = total + jnp.dot(left, amps[pair // 2], preferred_element_type=F32)
    mine = own_side[pair // 2]
    for tile, keep in ((tile_low, in_low), (tile_high, jnp.logical_not(in_low))):
        span = pl.ds(pl.multiple_of(tile * TILE, TILE), TILE)
        product = lax.dot_general(mine, fock[span, span], NT, preferred_element_type=F32)
        total = total + jnp.where(keep, product, jnp.zeros_like(product))
    out[...] = total


def final_kernel(place, lists, sums, local, out):
    pair, vir = place[0], place[1]
    rows = local.shape[0]
    low, high, in_low = row_tiles(lists, pair, vir, rows)
    chosen = jnp.where(in_low, lists[pair, low], lists[pair, high])
    total = local[...] + jnp.sum(sums[...].astype(F32), axis=0)
    for tile in range(out.shape[1] // TILE):
        out[:, tile * TILE : (tile + 1) * TILE] = jnp.where(chosen == tile, total, jnp.zeros_like(total))


SMEM = pl.BlockSpec(memory_space=pltpu.SMEM)
VMEM = pl.BlockSpec(memory_space=pltpu.VMEM)
ANY = pl.BlockSpec(memory_space=pl.ANY)


def shards(amplitudes, tile_list, ladder_factor, fock_vv, pair_coupling):
    rows, _, width = amplitudes.shape
    depth = ladder_factor.shape[0]
    z, core = lax.axis_index("z"), lax.axis_index("core")
    vir = lax.axis_index("x") * lax.axis_size("y") + lax.axis_index("y")
    pairs = lax.axis_size("z")
    peers = pairs * lax.axis_size("x") * lax.axis_size("y")
    swap = [(0, 1), (1, 0)]
    place = jnp.stack([2 * z + core, vir, core]).astype(jnp.int32)
    lists = tile_list[:, :, 0]
    tiles = lists.shape[1]

    other_factor = lax.ppermute(ladder_factor, "core", swap)
    repeated = pl.pallas_call(
        compact_kernel,
        in_specs=[SMEM, SMEM, VMEM],
        out_specs=VMEM,
        out_shape=jax.ShapeDtypeStruct((peers, rows, TILE), BF16),
        name="compact",
    )(place, lists, amplitudes.reshape(rows, width))
    gathered = lax.all_to_all(repeated, SAME_CORE, 0, 0, tiled=True)
    amps = gathered.reshape(pairs, width, TILE)
    own_side = lax.dynamic_index_in_dim(gathered.reshape(pairs, -1, rows, TILE), vir, 1, keepdims=False)
    other_side = lax.ppermute(own_side, "core", swap)

    partial_sums = pl.pallas_call(
        ladder_kernel,
        in_specs=[SMEM, SMEM, VMEM, ANY, ANY],
        out_specs=VMEM,
        out_shape=jax.ShapeDtypeStruct((pairs, width, TILE), F32),
        scratch_shapes=[
            pltpu.VMEM((2, depth, width, width), BF16),
            pltpu.VMEM((pairs * tiles, depth * width, TILE), BF16),
            pltpu.SMEM((pairs * tiles + 1,), jnp.int32),
            pltpu.SemaphoreType.DMA((2,)),
        ],
        compiler_params=pltpu.CompilerParams(vmem_limit_bytes=VMEM_LIMIT),
        cost_estimate=pl.CostEstimate(flops=17 * 10**9, bytes_accessed=20 * 10**6, transcendentals=0),
        name="ladder",
    )(place, lists, amps, ladder_factor, other_factor)

    local = pl.pallas_call(
        local_kernel,
        in_specs=[SMEM, SMEM, SMEM, VMEM, VMEM, VMEM, VMEM, VMEM],
        out_specs=VMEM,
        out_shape=jax.ShapeDtypeStruct((rows, TILE), F32),
        name="local_terms",
    )(place, lists, pair_coupling, own_side, other_side, amps, fock_vv.reshape(-1, rows, width), fock_vv)

    sent = partial_sums.astype(BF16).reshape(peers, rows, TILE)
    received = lax.all_to_all(sent, SAME_CORE, 0, 0, tiled=True)
    result = pl.pallas_call(
        final_kernel,
        in_specs=[SMEM, SMEM, VMEM, VMEM],
        out_specs=VMEM,
        out_shape=jax.ShapeDtypeStruct((rows, width), F32),
        name="final",
    )(place, lists, received, local)
    return result.reshape(rows, 1, width)


def solution(mesh):
    grid = Mesh(mesh.devices.reshape(4, 2, 4, 4), ("z", "core", "x", "y"))
    pairs_of, rows_of = ("z", "core"), ("x", "y")
    in_specs = (P(rows_of, pairs_of, None), P(), P(pairs_of + rows_of, None, None), P(), P())
    out_specs = P(rows_of, pairs_of, None)
    return jax.shard_map(shards, mesh=grid, in_specs=in_specs, out_specs=out_specs, check_vma=False)
```

```python
import jax
import jax.numpy as jnp
from jax import lax
from jax.experimental import pallas as pl
from jax.experimental.pallas import tpu as pltpu
from jax.sharding import Mesh
from jax.sharding import PartitionSpec as P

F32 = jnp.float32
BF16 = jnp.bfloat16
NT = (((1,), (1,)), ((), ()))
TILE = 128
SAME_CORE = ("z", "x", "y")
LADDER_VMEM = 60 << 20
SMALL_VMEM = 8 << 20
AT_ONCE = 4


def place():
    vir = lax.axis_index("x") * lax.axis_size("y") + lax.axis_index("y")
    return lax.axis_index("z") * 2 + lax.axis_index("core"), vir


def row_tiles(vir, rows):
    first = vir * rows
    low = first // TILE
    high = (first + rows - 1) // TILE
    index = lax.broadcasted_iota(jnp.int32, (rows, TILE), 0) + first
    return low, high, index < (low + 1) * TILE


def compact_kernel(lists, amps, out):
    pair, vir = place()
    rows, width = amps.shape
    low, high, in_low = row_tiles(vir, rows)
    chosen = jnp.where(in_low, lists[low, 0, pair], lists[high, 0, pair])
    kept = jnp.zeros((rows, TILE), F32)
    for tile in range(width // TILE):
        part = amps[:, tile * TILE : (tile + 1) * TILE].astype(F32)
        kept = jnp.where(chosen == tile, part, kept)
    out[...] = jnp.broadcast_to(kept.astype(BF16)[None], out.shape)


def ladder_kernel(lists, amps, own, other, out, factor, half, sums, items, sems):
    core = lax.axis_index("core")
    pairs, tiles = amps.shape[0], lists.shape[0]
    depth = own.shape[0]
    width = tiles * TILE

    def copy(source, chunk, tile):
        b_rows = pl.ds(tile * TILE, TILE)
        return pltpu.make_async_copy(source.at[:, b_rows, :], factor.at[chunk, :, b_rows, :], sems.at[chunk, tile])

    for tile in range(tiles):
        copy(own, 0, tile).start()
    count = jnp.int32(0)
    for tile in range(tiles):
        for pair in range(pairs):
            need = lists[0, 0, 2 * pair + core] == tile
            for row in range(1, tiles):
                need = need | (lists[row, 0, 2 * pair + core] == tile)
            items[count] = jnp.int32(pair * 8 + tile)
            count = count + need.astype(jnp.int32)
    sums[...] = jnp.zeros_like(sums)

    def half_of(chunk, index):
        item = items[index]
        pair, tile = item // 8, item % 8
        b_rows = pl.ds(pl.multiple_of(tile * TILE, TILE), TILE)
        for tile_c in range(tiles):
            start = pl.multiple_of(lists[tile_c, 0, 2 * pair + core] * TILE, TILE)
            panel = factor[chunk, :, b_rows, pl.ds(start, TILE)].reshape(depth * TILE, TILE)
            rows = amps[pair, tile_c * TILE : (tile_c + 1) * TILE, :]
            result = lax.dot_general(rows, panel, NT, preferred_element_type=F32).astype(BF16)
            for level in range(depth):
                first = level * width + tile_c * TILE
                half[pair * tiles + tile, first : first + TILE, :] = result[:, level * TILE : (level + 1) * TILE]

    def wait_up_to(chunk, arrived, last):
        for tile in range(tiles):

            @pl.when((arrived <= tile) & (last >= tile))
            def _():
                copy(own, chunk, tile).wait()

        return jnp.maximum(arrived, last + 1)

    def one_chunk(chunk, carry):
        def several(step, arrived):
            first = step * AT_ONCE
            arrived = wait_up_to(chunk, arrived, items[first + AT_ONCE - 1] % 8)
            for index in range(AT_ONCE):
                half_of(chunk, first + index)
            return arrived

        def one(index, carry):
            half_of(chunk, index)
            return carry

        steps = count // AT_ONCE
        arrived = lax.fori_loop(0, steps, several, jnp.int32(0))
        wait_up_to(chunk, arrived, jnp.int32(tiles - 1))
        lax.fori_loop(steps * AT_ONCE, count, one, 0)

        @pl.when(chunk == 0)
        def _():
            for tile in range(tiles):
                copy(other, 1, tile).start()

        for tile_a in range(tiles):
            a_rows = pl.ds(tile_a * TILE, TILE)
            left = jnp.concatenate([factor[chunk, level, a_rows, :] for level in range(depth)], axis=1)
            right = jnp.concatenate(
                [half[pair * tiles + lists[tile_a, 0, 2 * pair + core]] for pair in range(pairs)], axis=1
            )
            result = jnp.dot(left, right, preferred_element_type=F32)
            for pair in range(pairs):
                sums[pair, a_rows, :] += result[:, pair * TILE : (pair + 1) * TILE]
        return carry

    lax.fori_loop(0, 2, one_chunk, 0)
    out[...] = sums[...].astype(BF16)


def local_kernel(lists, coupling, own_side, other_side, amps, fock_rows, fock, out, tile_of_row):
    pair, vir = place()
    core = lax.axis_index("core")
    pairs, rows = own_side.shape[0], own_side.shape[1]
    tiles = lists.shape[0]
    low, high, in_low = row_tiles(vir, rows)
    tile_low, tile_high = lists[low, 0, pair], lists[high, 0, pair]
    total = jnp.zeros((rows, TILE), F32)
    for side, held in ((core, own_side), (1 - core, other_side)):
        for index in range(pairs):
            other = 2 * index + side
            weight = coupling[other, pair]
            none = jnp.float32(0)
            weight_low = jnp.where(lists[low, 0, other] == tile_low, weight, none)
            weight_high = jnp.where(lists[high, 0, other] == tile_high, weight, none)
            total = total + held[index].astype(F32) * jnp.where(in_low, weight_low, weight_high)
    chosen = jnp.where(in_low, tile_low, tile_high)
    masked = []
    for tile_c in range(tiles):
        part = fock_rows[vir, :, tile_c * TILE : (tile_c + 1) * TILE].astype(F32)
        masked.append(jnp.where(chosen == lists[tile_c, 0, pair], part, jnp.zeros_like(part)).astype(BF16))
    left = jnp.concatenate(masked, axis=1)
    total = total + jnp.dot(left, amps[pair // 2], preferred_element_type=F32)
    mine = own_side[pair // 2]
    for tile, keep in ((tile_low, in_low), (tile_high, jnp.logical_not(in_low))):
        span = pl.ds(pl.multiple_of(tile * TILE, TILE), TILE)
        product = lax.dot_general(mine, fock[span, span], NT, preferred_element_type=F32)
        total = total + jnp.where(keep, product, jnp.zeros_like(product))
    out[...] = total
    tile_of_row[...] = chosen


def final_kernel(sums, local, tile_of_row, out):
    chosen = tile_of_row[...]
    total = local[...] + jnp.sum(sums[...].astype(F32), axis=0)
    for tile in range(out.shape[2] // TILE):
        out[:, 0, tile * TILE : (tile + 1) * TILE] = jnp.where(chosen == tile, total, jnp.zeros_like(total))


SMEM = pl.BlockSpec(memory_space=pltpu.SMEM)
VMEM = pl.BlockSpec(memory_space=pltpu.VMEM)
ANY = pl.BlockSpec(memory_space=pl.ANY)


def shards(amplitudes, tile_list, ladder_factor, fock_vv, pair_coupling):
    rows, _, width = amplitudes.shape
    depth = ladder_factor.shape[0]
    pairs = lax.axis_size("z")
    vir_count = lax.axis_size("x") * lax.axis_size("y")
    peers = pairs * vir_count
    swap = [(0, 1), (1, 0)]
    lists = jnp.transpose(tile_list, (1, 2, 0))
    tiles = lists.shape[0]
    _, vir = place()

    other_factor = lax.ppermute(ladder_factor, "core", swap)
    repeated = pl.pallas_call(
        compact_kernel,
        in_specs=[SMEM, VMEM],
        out_specs=VMEM,
        out_shape=jax.ShapeDtypeStruct((peers, rows, TILE), BF16),
        name="compact",
    )(lists, amplitudes.reshape(rows, width))
    gathered = lax.all_to_all(repeated, SAME_CORE, 0, 0, tiled=True)
    amps = gathered.reshape(pairs, width, TILE)

    partial_sums = pl.pallas_call(
        ladder_kernel,
        in_specs=[SMEM, VMEM, ANY, ANY],
        out_specs=VMEM,
        out_shape=jax.ShapeDtypeStruct((pairs, width, TILE), BF16),
        scratch_shapes=[
            pltpu.VMEM((2, depth, width, width), BF16),
            pltpu.VMEM((pairs * tiles, depth * width, TILE), BF16),
            pltpu.VMEM((pairs, width, TILE), F32),
            pltpu.SMEM((pairs * tiles + 1,), jnp.int32),
            pltpu.SemaphoreType.DMA((2, tiles)),
        ],
        compiler_params=pltpu.CompilerParams(vmem_limit_bytes=LADDER_VMEM),
        cost_estimate=pl.CostEstimate(flops=17 * 10**9, bytes_accessed=20 * 10**6, transcendentals=0),
        name="ladder",
    )(lists, amps, ladder_factor, other_factor)

    own_side = lax.dynamic_index_in_dim(gathered.reshape(pairs, vir_count, rows, TILE), vir, 1, keepdims=False)
    other_side = lax.ppermute(own_side, "core", swap)
    local, tile_of_row = pl.pallas_call(
        local_kernel,
        in_specs=[SMEM, SMEM, VMEM, VMEM, VMEM, VMEM, VMEM],
        out_specs=(VMEM, VMEM),
        out_shape=(
            jax.ShapeDtypeStruct((rows, TILE), F32),
            jax.ShapeDtypeStruct((rows, TILE), jnp.int32),
        ),
        compiler_params=pltpu.CompilerParams(vmem_limit_bytes=SMALL_VMEM),
        name="local_terms",
    )(lists, pair_coupling, own_side, other_side, amps, fock_vv.reshape(vir_count, rows, width), fock_vv)

    received = lax.all_to_all(partial_sums.reshape(peers, rows, TILE), SAME_CORE, 0, 0, tiled=True)
    return pl.pallas_call(
        final_kernel,
        in_specs=[VMEM, VMEM, VMEM],
        out_specs=VMEM,
        out_shape=jax.ShapeDtypeStruct((rows, 1, width), F32),
        compiler_params=pltpu.CompilerParams(vmem_limit_bytes=SMALL_VMEM),
        name="final",
    )(received, local, tile_of_row)


def solution(mesh):
    grid = Mesh(mesh.devices.reshape(4, 2, 4, 4), ("z", "core", "x", "y"))
    pairs_of, rows_of = ("z", "core"), ("x", "y")
    in_specs = (P(rows_of, pairs_of, None), P(), P(pairs_of + rows_of, None, None), P(), P())
    out_specs = P(rows_of, pairs_of, None)
    return jax.shard_map(shards, mesh=grid, in_specs=in_specs, out_specs=out_specs, check_vma=False)
```

```python
import jax
import jax.numpy as jnp
from jax import lax
from jax.experimental import pallas as pl
from jax.experimental.pallas import tpu as pltpu
from jax.sharding import Mesh
from jax.sharding import PartitionSpec as P

F32 = jnp.float32
BF16 = jnp.bfloat16
NT = (((1,), (1,)), ((), ()))
TILE = 128
SAME_CORE = ("z", "x", "y")
LADDER_VMEM = 57 << 20
SMALL_VMEM = 8 << 20
COMPACT_VMEM = 57 << 20
AT_ONCE = 4


def place():
    vir = lax.axis_index("x") * lax.axis_size("y") + lax.axis_index("y")
    return lax.axis_index("z") * 2 + lax.axis_index("core"), vir


def row_tiles(vir, rows):
    first = vir * rows
    low = first // TILE
    high = (first + rows - 1) // TILE
    index = lax.broadcasted_iota(jnp.int32, (rows, TILE), 0) + first
    return low, high, index < (low + 1) * TILE


def compact_kernel(lists, amps, out):
    pair, vir = place()
    rows, width = amps.shape
    low, high, in_low = row_tiles(vir, rows)
    chosen = jnp.where(in_low, lists[low, 0, pair], lists[high, 0, pair])
    kept = jnp.zeros((rows, TILE), F32)
    for tile in range(width // TILE):
        part = amps[:, tile * TILE : (tile + 1) * TILE].astype(F32)
        kept = jnp.where(chosen == tile, part, kept)
    out[...] = jnp.broadcast_to(kept.astype(BF16)[None], out.shape)


def ladder_kernel(lists, amps, own, other, out, factor, half, sums, items, sems):
    core = lax.axis_index("core")
    pairs, tiles = amps.shape[0], lists.shape[0]
    depth = own.shape[0]
    width = tiles * TILE

    def copy(source, chunk, tile):
        b_rows = pl.ds(tile * TILE, TILE)
        return pltpu.make_async_copy(source.at[:, b_rows, :], factor.at[chunk, :, b_rows, :], sems.at[chunk, tile])

    for tile in range(tiles):
        copy(own, 0, tile).start()
    count = jnp.int32(0)
    for tile in range(tiles):
        for pair in range(pairs):
            need = lists[0, 0, 2 * pair + core] == tile
            for row in range(1, tiles):
                need = need | (lists[row, 0, 2 * pair + core] == tile)
            items[count] = jnp.int32(pair * 8 + tile)
            count = count + need.astype(jnp.int32)
    sums[...] = jnp.zeros_like(sums)

    def half_of(chunk, index):
        item = items[index]
        pair, tile = item // 8, item % 8
        b_rows = pl.ds(pl.multiple_of(tile * TILE, TILE), TILE)
        for tile_c in range(tiles):
            start = pl.multiple_of(lists[tile_c, 0, 2 * pair + core] * TILE, TILE)
            panel = factor[chunk, :, b_rows, pl.ds(start, TILE)].reshape(depth * TILE, TILE)
            rows = amps[pair, tile_c * TILE : (tile_c + 1) * TILE, :]
            result = lax.dot_general(rows, panel, NT, preferred_element_type=F32).astype(BF16)
            for level in range(depth):
                first = level * width + tile_c * TILE
                half[pair * tiles + tile, first : first + TILE, :] = result[:, level * TILE : (level + 1) * TILE]

    def wait_up_to(chunk, arrived, last):
        for tile in range(tiles):

            @pl.when((arrived <= tile) & (last >= tile))
            def _():
                copy(own, chunk, tile).wait()

        return jnp.maximum(arrived, last + 1)

    def one_chunk(chunk, carry):
        def several(step, arrived):
            first = step * AT_ONCE
            arrived = wait_up_to(chunk, arrived, items[first + AT_ONCE - 1] % 8)
            for index in range(AT_ONCE):
                half_of(chunk, first + index)
            return arrived

        def one(index, carry):
            half_of(chunk, index)
            return carry

        steps = count // AT_ONCE
        arrived = lax.fori_loop(0, steps, several, jnp.int32(0))
        wait_up_to(chunk, arrived, jnp.int32(tiles - 1))
        lax.fori_loop(steps * AT_ONCE, count, one, 0)

        @pl.when(chunk == 0)
        def _():
            for tile in range(tiles):
                copy(other, 1, tile).start()

        for tile_a in range(tiles):
            a_rows = pl.ds(tile_a * TILE, TILE)
            left = jnp.concatenate([factor[chunk, level, a_rows, :] for level in range(depth)], axis=1)
            right = jnp.concatenate(
                [half[pair * tiles + lists[tile_a, 0, 2 * pair + core]] for pair in range(pairs)], axis=1
            )
            result = jnp.dot(left, right, preferred_element_type=F32)
            for pair in range(pairs):
                sums[pair, a_rows, :] += result[:, pair * TILE : (pair + 1) * TILE]
        return carry

    lax.fori_loop(0, 2, one_chunk, 0)
    out[...] = sums[...].astype(BF16)


def local_kernel(lists, coupling, own_side, other_side, amps, fock_rows, fock, out, tile_of_row):
    pair, vir = place()
    core = lax.axis_index("core")
    pairs, rows = own_side.shape[0], own_side.shape[1]
    tiles = lists.shape[0]
    low, high, in_low = row_tiles(vir, rows)
    tile_low, tile_high = lists[low, 0, pair], lists[high, 0, pair]
    total = jnp.zeros((rows, TILE), F32)
    for side, held in ((core, own_side), (1 - core, other_side)):
        for index in range(pairs):
            other = 2 * index + side
            weight = coupling[other, pair]
            none = jnp.float32(0)
            weight_low = jnp.where(lists[low, 0, other] == tile_low, weight, none)
            weight_high = jnp.where(lists[high, 0, other] == tile_high, weight, none)
            total = total + held[index].astype(F32) * jnp.where(in_low, weight_low, weight_high)
    chosen = jnp.where(in_low, tile_low, tile_high)
    masked = []
    for tile_c in range(tiles):
        part = fock_rows[vir, :, tile_c * TILE : (tile_c + 1) * TILE].astype(F32)
        masked.append(jnp.where(chosen == lists[tile_c, 0, pair], part, jnp.zeros_like(part)).astype(BF16))
    left = jnp.concatenate(masked, axis=1)
    total = total + jnp.dot(left, amps[pair // 2], preferred_element_type=F32)
    mine = own_side[pair // 2]
    for tile, keep in ((tile_low, in_low), (tile_high, jnp.logical_not(in_low))):
        span = pl.ds(pl.multiple_of(tile * TILE, TILE), TILE)
        product = lax.dot_general(mine, fock[span, span], NT, preferred_element_type=F32)
        total = total + jnp.where(keep, product, jnp.zeros_like(product))
    out[...] = total
    tile_of_row[...] = chosen


def final_kernel(sums, local, tile_of_row, out):
    chosen = tile_of_row[...]
    total = local[...] + jnp.sum(sums[...].astype(F32), axis=0)
    for tile in range(out.shape[2] // TILE):
        out[:, 0, tile * TILE : (tile + 1) * TILE] = jnp.where(chosen == tile, total, jnp.zeros_like(total))


SMEM = pl.BlockSpec(memory_space=pltpu.SMEM)
VMEM = pl.BlockSpec(memory_space=pltpu.VMEM)
ANY = pl.BlockSpec(memory_space=pl.ANY)


def in_hbm(array):
    return pltpu.with_memory_space_constraint(array, pltpu.HBM)


def in_vmem(array):
    return pltpu.with_memory_space_constraint(array, pltpu.VMEM)


def shards(amplitudes, tile_list, ladder_factor, fock_vv, pair_coupling):
    rows, _, width = amplitudes.shape
    depth = ladder_factor.shape[0]
    pairs = lax.axis_size("z")
    vir_count = lax.axis_size("x") * lax.axis_size("y")
    peers = pairs * vir_count
    swap = [(0, 1), (1, 0)]
    lists = jnp.transpose(tile_list, (1, 2, 0))
    tiles = lists.shape[0]
    _, vir = place()

    other_factor = lax.ppermute(ladder_factor, "core", swap)
    repeated = pl.pallas_call(
        compact_kernel,
        in_specs=[SMEM, VMEM],
        out_specs=VMEM,
        out_shape=pltpu.VMEM((peers, rows, TILE), BF16),
        compiler_params=pltpu.CompilerParams(vmem_limit_bytes=COMPACT_VMEM),
        name="compact",
    )(in_hbm(lists), in_hbm(amplitudes.reshape(rows, width)))
    gathered = lax.all_to_all(repeated, SAME_CORE, 0, 0, tiled=True)
    amps = gathered.reshape(pairs, width, TILE)

    partial_sums = pl.pallas_call(
        ladder_kernel,
        in_specs=[SMEM, VMEM, ANY, ANY],
        out_specs=VMEM,
        out_shape=pltpu.VMEM((pairs, width, TILE), BF16),
        scratch_shapes=[
            pltpu.VMEM((2, depth, width, width), BF16),
            pltpu.VMEM((pairs * tiles, depth * width, TILE), BF16),
            pltpu.VMEM((pairs, width, TILE), F32),
            pltpu.SMEM((pairs * tiles + 1,), jnp.int32),
            pltpu.SemaphoreType.DMA((2, tiles)),
        ],
        compiler_params=pltpu.CompilerParams(vmem_limit_bytes=LADDER_VMEM),
        cost_estimate=pl.CostEstimate(flops=17 * 10**9, bytes_accessed=20 * 10**6, transcendentals=0),
        name="ladder",
    )(in_hbm(lists), in_vmem(amps), in_hbm(ladder_factor), in_hbm(other_factor))

    own_side = lax.dynamic_index_in_dim(gathered.reshape(pairs, vir_count, rows, TILE), vir, 1, keepdims=False)
    other_side = lax.ppermute(own_side, "core", swap)
    local, tile_of_row = pl.pallas_call(
        local_kernel,
        in_specs=[SMEM, SMEM, VMEM, VMEM, VMEM, VMEM, VMEM],
        out_specs=(VMEM, VMEM),
        out_shape=(
            jax.ShapeDtypeStruct((rows, TILE), F32),
            jax.ShapeDtypeStruct((rows, TILE), jnp.int32),
        ),
        compiler_params=pltpu.CompilerParams(vmem_limit_bytes=SMALL_VMEM),
        name="local_terms",
    )(lists, pair_coupling, own_side, other_side, amps, fock_vv.reshape(vir_count, rows, width), fock_vv)

    received = lax.all_to_all(partial_sums.reshape(peers, rows, TILE), SAME_CORE, 0, 0, tiled=True)
    return pl.pallas_call(
        final_kernel,
        in_specs=[VMEM, VMEM, VMEM],
        out_specs=VMEM,
        out_shape=jax.ShapeDtypeStruct((rows, 1, width), F32),
        compiler_params=pltpu.CompilerParams(vmem_limit_bytes=SMALL_VMEM),
        name="final",
    )(received, local, tile_of_row)


def solution(mesh):
    grid = Mesh(mesh.devices.reshape(4, 2, 4, 4), ("z", "core", "x", "y"))
    pairs_of, rows_of = ("z", "core"), ("x", "y")
    in_specs = (P(rows_of, pairs_of, None), P(), P(pairs_of + rows_of, None, None), P(), P())
    out_specs = P(rows_of, pairs_of, None)
    return jax.shard_map(shards, mesh=grid, in_specs=in_specs, out_specs=out_specs, check_vma=False)
```

```python
import jax
import jax.numpy as jnp
from jax import lax
from jax.experimental import pallas as pl
from jax.experimental.pallas import tpu as pltpu
from jax.sharding import Mesh
from jax.sharding import PartitionSpec as P

F32 = jnp.float32
BF16 = jnp.bfloat16
NT = (((1,), (1,)), ((), ()))
TILE = 128
SAME_CORE = ("z", "x", "y")
LADDER_VMEM = 57 << 20
SMALL_VMEM = 8 << 20
COMPACT_VMEM = 57 << 20
AT_ONCE = 8


def place():
    vir = lax.axis_index("x") * lax.axis_size("y") + lax.axis_index("y")
    return lax.axis_index("z") * 2 + lax.axis_index("core"), vir


def row_tiles(vir, rows):
    first = vir * rows
    low = first // TILE
    high = (first + rows - 1) // TILE
    index = lax.broadcasted_iota(jnp.int32, (rows, TILE), 0) + first
    return low, high, index < (low + 1) * TILE


def compact_kernel(lists, amps, out):
    pair, vir = place()
    rows, width = amps.shape
    low, high, in_low = row_tiles(vir, rows)
    chosen = jnp.where(in_low, lists[low, 0, pair], lists[high, 0, pair])
    kept = jnp.zeros((rows, TILE), F32)
    for tile in range(width // TILE):
        part = amps[:, tile * TILE : (tile + 1) * TILE].astype(F32)
        kept = jnp.where(chosen == tile, part, kept)
    out[...] = jnp.broadcast_to(kept.astype(BF16)[None], out.shape)


def ladder_kernel(lists, amps, own, other, out, factor, half, sums, items, sems):
    core = lax.axis_index("core")
    pairs, tiles = amps.shape[0], lists.shape[0]
    depth = own.shape[0]
    width = tiles * TILE

    def copy(source, chunk, tile):
        b_rows = pl.ds(tile * TILE, TILE)
        return pltpu.make_async_copy(source.at[:, b_rows, :], factor.at[chunk, :, b_rows, :], sems.at[chunk, tile])

    for tile in range(tiles):
        copy(own, 0, tile).start()
    count = jnp.int32(0)
    for tile in range(tiles):
        for pair in range(pairs):
            need = lists[0, 0, 2 * pair + core] == tile
            for row in range(1, tiles):
                need = need | (lists[row, 0, 2 * pair + core] == tile)
            items[count] = jnp.int32(pair * 8 + tile)
            count = count + need.astype(jnp.int32)
    sums[...] = jnp.zeros_like(sums)

    def half_of(chunk, index):
        item = items[index]
        pair, tile = item // 8, item % 8
        b_rows = pl.ds(pl.multiple_of(tile * TILE, TILE), TILE)
        for tile_c in range(tiles):
            start = pl.multiple_of(lists[tile_c, 0, 2 * pair + core] * TILE, TILE)
            panel = factor[chunk, :, b_rows, pl.ds(start, TILE)].reshape(depth * TILE, TILE)
            rows = amps[pair, tile_c * TILE : (tile_c + 1) * TILE, :]
            result = lax.dot_general(rows, panel, NT, preferred_element_type=F32).astype(BF16)
            for level in range(depth):
                first = level * width + tile_c * TILE
                half[pair * tiles + tile, first : first + TILE, :] = result[:, level * TILE : (level + 1) * TILE]

    def wait_up_to(chunk, arrived, last):
        for tile in range(tiles):

            @pl.when((arrived <= tile) & (last >= tile))
            def _():
                copy(own, chunk, tile).wait()

        return jnp.maximum(arrived, last + 1)

    def one_chunk(chunk, carry):
        def several(first, size, arrived):
            arrived = wait_up_to(chunk, arrived, items[first + size - 1] % 8)
            for index in range(size):
                half_of(chunk, first + index)
            return arrived

        first, arrived, size = jnp.int32(0), jnp.int32(0), 1
        while size < AT_ONCE:
            odd = (count // size) % 2 == 1
            last = jnp.where(odd, items[jnp.minimum(first + size, count) - 1] % 8, -1)
            arrived = wait_up_to(chunk, arrived, last)

            @pl.when(odd)
            def _():
                for index in range(size):
                    half_of(chunk, first + index)

            first = jnp.where(odd, first + size, first)
            size *= 2
        arrived = lax.fori_loop(
            0, count // AT_ONCE, lambda step, seen: several(first + step * AT_ONCE, AT_ONCE, seen), arrived
        )
        wait_up_to(chunk, arrived, jnp.int32(tiles - 1))

        @pl.when(chunk == 0)
        def _():
            for tile in range(tiles):
                copy(other, 1, tile).start()

        for tile_a in range(tiles):
            a_rows = pl.ds(tile_a * TILE, TILE)
            left = jnp.concatenate([factor[chunk, level, a_rows, :] for level in range(depth)], axis=1)
            right = jnp.concatenate(
                [half[pair * tiles + lists[tile_a, 0, 2 * pair + core]] for pair in range(pairs)], axis=1
            )
            result = jnp.dot(left, right, preferred_element_type=F32)
            for pair in range(pairs):
                sums[pair, a_rows, :] += result[:, pair * TILE : (pair + 1) * TILE]
        return carry

    lax.fori_loop(0, 2, one_chunk, 0)
    out[...] = sums[...].astype(BF16)


def local_kernel(lists, coupling, own_side, other_side, amps, fock_rows, fock, out, tile_of_row):
    pair, vir = place()
    core = lax.axis_index("core")
    pairs, rows = own_side.shape[0], own_side.shape[1]
    tiles = lists.shape[0]
    low, high, in_low = row_tiles(vir, rows)
    tile_low, tile_high = lists[low, 0, pair], lists[high, 0, pair]
    total = jnp.zeros((rows, TILE), F32)
    for side, held in ((core, own_side), (1 - core, other_side)):
        for index in range(pairs):
            other = 2 * index + side
            weight = coupling[other, pair]
            none = jnp.float32(0)
            weight_low = jnp.where(lists[low, 0, other] == tile_low, weight, none)
            weight_high = jnp.where(lists[high, 0, other] == tile_high, weight, none)
            total = total + held[index].astype(F32) * jnp.where(in_low, weight_low, weight_high)
    chosen = jnp.where(in_low, tile_low, tile_high)
    masked = []
    for tile_c in range(tiles):
        part = fock_rows[vir, :, tile_c * TILE : (tile_c + 1) * TILE].astype(F32)
        masked.append(jnp.where(chosen == lists[tile_c, 0, pair], part, jnp.zeros_like(part)).astype(BF16))
    left = jnp.concatenate(masked, axis=1)
    total = total + jnp.dot(left, amps[pair // 2], preferred_element_type=F32)
    mine = own_side[pair // 2]
    for tile, keep in ((tile_low, in_low), (tile_high, jnp.logical_not(in_low))):
        span = pl.ds(pl.multiple_of(tile * TILE, TILE), TILE)
        product = lax.dot_general(mine, fock[span, span], NT, preferred_element_type=F32)
        total = total + jnp.where(keep, product, jnp.zeros_like(product))
    out[...] = total
    tile_of_row[...] = chosen


def final_kernel(sums, local, tile_of_row, out):
    chosen = tile_of_row[...]
    total = local[...] + jnp.sum(sums[...].astype(F32), axis=0)
    for tile in range(out.shape[2] // TILE):
        out[:, 0, tile * TILE : (tile + 1) * TILE] = jnp.where(chosen == tile, total, jnp.zeros_like(total))


SMEM = pl.BlockSpec(memory_space=pltpu.SMEM)
VMEM = pl.BlockSpec(memory_space=pltpu.VMEM)
ANY = pl.BlockSpec(memory_space=pl.ANY)


def in_hbm(array):
    return pltpu.with_memory_space_constraint(array, pltpu.HBM)


def in_vmem(array):
    return pltpu.with_memory_space_constraint(array, pltpu.VMEM)


def shards(amplitudes, tile_list, ladder_factor, fock_vv, pair_coupling):
    rows, _, width = amplitudes.shape
    depth = ladder_factor.shape[0]
    pairs = lax.axis_size("z")
    vir_count = lax.axis_size("x") * lax.axis_size("y")
    peers = pairs * vir_count
    swap = [(0, 1), (1, 0)]
    lists = jnp.transpose(tile_list, (1, 2, 0))
    tiles = lists.shape[0]
    _, vir = place()

    other_factor = lax.ppermute(ladder_factor, "core", swap)
    repeated = pl.pallas_call(
        compact_kernel,
        in_specs=[SMEM, VMEM],
        out_specs=VMEM,
        out_shape=pltpu.VMEM((peers, rows, TILE), BF16),
        compiler_params=pltpu.CompilerParams(vmem_limit_bytes=COMPACT_VMEM),
        name="compact",
    )(in_hbm(lists), in_hbm(amplitudes.reshape(rows, width)))
    gathered = lax.all_to_all(repeated, SAME_CORE, 0, 0, tiled=True)
    amps = gathered.reshape(pairs, width, TILE)

    partial_sums = pl.pallas_call(
        ladder_kernel,
        in_specs=[SMEM, VMEM, ANY, ANY],
        out_specs=VMEM,
        out_shape=pltpu.VMEM((pairs, width, TILE), BF16),
        scratch_shapes=[
            pltpu.VMEM((2, depth, width, width), BF16),
            pltpu.VMEM((pairs * tiles, depth * width, TILE), BF16),
            pltpu.VMEM((pairs, width, TILE), F32),
            pltpu.SMEM((pairs * tiles + 1,), jnp.int32),
            pltpu.SemaphoreType.DMA((2, tiles)),
        ],
        compiler_params=pltpu.CompilerParams(vmem_limit_bytes=LADDER_VMEM),
        cost_estimate=pl.CostEstimate(flops=17 * 10**9, bytes_accessed=20 * 10**6, transcendentals=0),
        name="ladder",
    )(in_hbm(lists), in_vmem(amps), in_hbm(ladder_factor), in_hbm(other_factor))

    own_side = lax.dynamic_index_in_dim(gathered.reshape(pairs, vir_count, rows, TILE), vir, 1, keepdims=False)
    other_side = lax.ppermute(own_side, "core", swap)
    local, tile_of_row = pl.pallas_call(
        local_kernel,
        in_specs=[SMEM, SMEM, VMEM, VMEM, VMEM, VMEM, VMEM],
        out_specs=(VMEM, VMEM),
        out_shape=(
            jax.ShapeDtypeStruct((rows, TILE), F32),
            jax.ShapeDtypeStruct((rows, TILE), jnp.int32),
        ),
        compiler_params=pltpu.CompilerParams(vmem_limit_bytes=SMALL_VMEM),
        name="local_terms",
    )(lists, pair_coupling, own_side, other_side, amps, fock_vv.reshape(vir_count, rows, width), fock_vv)

    received = lax.all_to_all(partial_sums.reshape(peers, rows, TILE), SAME_CORE, 0, 0, tiled=True)
    return pl.pallas_call(
        final_kernel,
        in_specs=[VMEM, VMEM, VMEM],
        out_specs=VMEM,
        out_shape=jax.ShapeDtypeStruct((rows, 1, width), F32),
        compiler_params=pltpu.CompilerParams(vmem_limit_bytes=SMALL_VMEM),
        name="final",
    )(received, local, tile_of_row)


def solution(mesh):
    grid = Mesh(mesh.devices.reshape(4, 2, 4, 4), ("z", "core", "x", "y"))
    pairs_of, rows_of = ("z", "core"), ("x", "y")
    in_specs = (P(rows_of, pairs_of, None), P(), P(pairs_of + rows_of, None, None), P(), P())
    out_specs = P(rows_of, pairs_of, None)
    return jax.shard_map(shards, mesh=grid, in_specs=in_specs, out_specs=out_specs, check_vma=False)
```

```python
import jax
import jax.numpy as jnp
from jax import lax
from jax.experimental import pallas as pl
from jax.experimental.pallas import tpu as pltpu
from jax.sharding import Mesh
from jax.sharding import PartitionSpec as P

F32 = jnp.float32
BF16 = jnp.bfloat16
NT = (((1,), (1,)), ((), ()))
TILE = 128
SAME_CORE = ("z", "x", "y")
LADDER_VMEM = 57 << 20
SMALL_VMEM = 8 << 20
COMPACT_VMEM = 57 << 20
AT_ONCE = 8


def place():
    vir = lax.axis_index("x") * lax.axis_size("y") + lax.axis_index("y")
    return lax.axis_index("z") * 2 + lax.axis_index("core"), vir


def row_tiles(vir, rows):
    first = vir * rows
    low = first // TILE
    high = (first + rows - 1) // TILE
    index = lax.broadcasted_iota(jnp.int32, (rows, TILE), 0) + first
    return low, high, index < (low + 1) * TILE


def compact_kernel(lists, amps, out):
    pair, vir = place()
    rows, width = amps.shape
    low, high, in_low = row_tiles(vir, rows)
    chosen = jnp.where(in_low, lists[low, 0, pair], lists[high, 0, pair])
    kept = jnp.zeros((rows, TILE), F32)
    for tile in range(width // TILE):
        part = amps[:, tile * TILE : (tile + 1) * TILE].astype(F32)
        kept = jnp.where(chosen == tile, part, kept)
    out[...] = jnp.broadcast_to(kept.astype(BF16)[None], out.shape)


def ladder_kernel(lists_in, amps, own, other, out, lists, factor, half, sums, items, sems, list_sem):
    core = lax.axis_index("core")
    pairs, tiles = amps.shape[0], lists.shape[0]
    depth = own.shape[0]
    width = tiles * TILE

    def copy(source, chunk, tile):
        b_rows = pl.ds(pl.multiple_of(tile * TILE, TILE), TILE)
        return pltpu.make_async_copy(source.at[:, b_rows, :], factor.at[chunk, :, b_rows, :], sems.at[chunk, tile])

    for tile in range(tiles):
        copy(own, 0, tile).start()
        if tile == 0:
            list_copy = pltpu.make_async_copy(lists_in, lists, list_sem)
            list_copy.start()
    list_copy.wait()
    count = jnp.int32(0)
    for tile in range(tiles):
        for pair in range(pairs):
            need = lists[0, 0, 2 * pair + core] == tile
            for row in range(1, tiles):
                need = need | (lists[row, 0, 2 * pair + core] == tile)
            items[count] = jnp.int32(pair * 8 + tile)
            count = count + need.astype(jnp.int32)
    sums[...] = jnp.zeros_like(sums)

    def half_of(chunk, index):
        item = items[index]
        pair, tile = item // 8, item % 8
        b_rows = pl.ds(pl.multiple_of(tile * TILE, TILE), TILE)
        for tile_c in range(tiles):
            start = pl.multiple_of(lists[tile_c, 0, 2 * pair + core] * TILE, TILE)
            panel = factor[chunk, :, b_rows, pl.ds(start, TILE)].reshape(depth * TILE, TILE)
            rows = amps[pair, tile_c * TILE : (tile_c + 1) * TILE, :]
            result = lax.dot_general(rows, panel, NT, preferred_element_type=F32).astype(BF16)
            for level in range(depth):
                first = level * width + tile_c * TILE
                half[pair * tiles + tile, first : first + TILE, :] = result[:, level * TILE : (level + 1) * TILE]

    def wait_up_to(chunk, arrived, last):
        def one(tile, carry):
            copy(own, chunk, tile).wait()
            return carry

        lax.fori_loop(arrived, last + 1, one, 0)
        return jnp.maximum(arrived, last + 1)

    def one_chunk(chunk, carry):
        def several(first, size, arrived):
            arrived = wait_up_to(chunk, arrived, items[first + size - 1] % 8)
            for index in range(size):
                half_of(chunk, first + index)
            return arrived

        first, arrived, size = jnp.int32(0), jnp.int32(0), 1
        while size < AT_ONCE:
            odd = (count // size) % 2 == 1
            last = jnp.where(odd, items[jnp.minimum(first + size, count) - 1] % 8, -1)
            arrived = wait_up_to(chunk, arrived, last)

            @pl.when(odd)
            def _():
                for index in range(size):
                    half_of(chunk, first + index)

            first = jnp.where(odd, first + size, first)
            size *= 2
        arrived = lax.fori_loop(
            0, count // AT_ONCE, lambda step, seen: several(first + step * AT_ONCE, AT_ONCE, seen), arrived
        )
        wait_up_to(chunk, arrived, jnp.int32(tiles - 1))

        @pl.when(chunk == 0)
        def _():
            for tile in range(tiles):
                copy(other, 1, tile).start()

        for tile_a in range(tiles):
            a_rows = pl.ds(tile_a * TILE, TILE)
            left = jnp.concatenate([factor[chunk, level, a_rows, :] for level in range(depth)], axis=1)
            right = jnp.concatenate(
                [half[pair * tiles + lists[tile_a, 0, 2 * pair + core]] for pair in range(pairs)], axis=1
            )
            result = jnp.dot(left, right, preferred_element_type=F32)
            for pair in range(pairs):
                sums[pair, a_rows, :] += result[:, pair * TILE : (pair + 1) * TILE]
        return carry

    lax.fori_loop(0, 2, one_chunk, 0)
    out[...] = sums[...].astype(BF16)


def local_kernel(lists, coupling, own_side, other_side, amps, fock_rows, fock, out, tile_of_row):
    pair, vir = place()
    core = lax.axis_index("core")
    pairs, rows = own_side.shape[0], own_side.shape[1]
    tiles = lists.shape[0]
    low, high, in_low = row_tiles(vir, rows)
    tile_low, tile_high = lists[low, 0, pair], lists[high, 0, pair]
    total = jnp.zeros((rows, TILE), F32)
    for side, held in ((core, own_side), (1 - core, other_side)):
        for index in range(pairs):
            other = 2 * index + side
            weight = coupling[other, pair]
            none = jnp.float32(0)
            weight_low = jnp.where(lists[low, 0, other] == tile_low, weight, none)
            weight_high = jnp.where(lists[high, 0, other] == tile_high, weight, none)
            total = total + held[index].astype(F32) * jnp.where(in_low, weight_low, weight_high)
    chosen = jnp.where(in_low, tile_low, tile_high)
    masked = []
    for tile_c in range(tiles):
        part = fock_rows[vir, :, tile_c * TILE : (tile_c + 1) * TILE].astype(F32)
        masked.append(jnp.where(chosen == lists[tile_c, 0, pair], part, jnp.zeros_like(part)).astype(BF16))
    left = jnp.concatenate(masked, axis=1)
    total = total + jnp.dot(left, amps[pair // 2], preferred_element_type=F32)
    mine = own_side[pair // 2]
    for tile, keep in ((tile_low, in_low), (tile_high, jnp.logical_not(in_low))):
        span = pl.ds(pl.multiple_of(tile * TILE, TILE), TILE)
        product = lax.dot_general(mine, fock[span, span], NT, preferred_element_type=F32)
        total = total + jnp.where(keep, product, jnp.zeros_like(product))
    out[...] = total
    tile_of_row[...] = chosen


def final_kernel(sums, local, tile_of_row, out):
    chosen = tile_of_row[...]
    total = local[...] + jnp.sum(sums[...].astype(F32), axis=0)
    for tile in range(out.shape[2] // TILE):
        out[:, 0, tile * TILE : (tile + 1) * TILE] = jnp.where(chosen == tile, total, jnp.zeros_like(total))


SMEM = pl.BlockSpec(memory_space=pltpu.SMEM)
VMEM = pl.BlockSpec(memory_space=pltpu.VMEM)
ANY = pl.BlockSpec(memory_space=pl.ANY)


def in_hbm(array):
    return pltpu.with_memory_space_constraint(array, pltpu.HBM)


def in_vmem(array):
    return pltpu.with_memory_space_constraint(array, pltpu.VMEM)


def shards(amplitudes, tile_list, ladder_factor, fock_vv, pair_coupling):
    rows, _, width = amplitudes.shape
    depth = ladder_factor.shape[0]
    pairs = lax.axis_size("z")
    vir_count = lax.axis_size("x") * lax.axis_size("y")
    peers = pairs * vir_count
    swap = [(0, 1), (1, 0)]
    lists = jnp.transpose(tile_list, (1, 2, 0))
    tiles = lists.shape[0]
    _, vir = place()

    other_factor = lax.ppermute(ladder_factor, "core", swap)
    repeated = pl.pallas_call(
        compact_kernel,
        in_specs=[SMEM, VMEM],
        out_specs=VMEM,
        out_shape=pltpu.VMEM((peers, rows, TILE), BF16),
        compiler_params=pltpu.CompilerParams(vmem_limit_bytes=COMPACT_VMEM),
        name="compact",
    )(in_hbm(lists), in_hbm(amplitudes.reshape(rows, width)))
    gathered = lax.all_to_all(repeated, SAME_CORE, 0, 0, tiled=True)
    amps = gathered.reshape(pairs, width, TILE)

    partial_sums = pl.pallas_call(
        ladder_kernel,
        in_specs=[ANY, VMEM, ANY, ANY],
        out_specs=VMEM,
        out_shape=pltpu.VMEM((pairs, width, TILE), BF16),
        scratch_shapes=[
            pltpu.SMEM(lists.shape, jnp.int32),
            pltpu.VMEM((2, depth, width, width), BF16),
            pltpu.VMEM((pairs * tiles, depth * width, TILE), BF16),
            pltpu.VMEM((pairs, width, TILE), F32),
            pltpu.SMEM((pairs * tiles + 1,), jnp.int32),
            pltpu.SemaphoreType.DMA((2, tiles)),
            pltpu.SemaphoreType.DMA,
        ],
        compiler_params=pltpu.CompilerParams(vmem_limit_bytes=LADDER_VMEM),
        cost_estimate=pl.CostEstimate(flops=17 * 10**9, bytes_accessed=20 * 10**6, transcendentals=0),
        name="ladder",
    )(in_hbm(lists), in_vmem(amps), in_hbm(ladder_factor), in_hbm(other_factor))

    own_side = lax.dynamic_index_in_dim(gathered.reshape(pairs, vir_count, rows, TILE), vir, 1, keepdims=False)
    other_side = lax.ppermute(own_side, "core", swap)
    local, tile_of_row = pl.pallas_call(
        local_kernel,
        in_specs=[SMEM, SMEM, VMEM, VMEM, VMEM, VMEM, VMEM],
        out_specs=(VMEM, VMEM),
        out_shape=(
            jax.ShapeDtypeStruct((rows, TILE), F32),
            jax.ShapeDtypeStruct((rows, TILE), jnp.int32),
        ),
        compiler_params=pltpu.CompilerParams(vmem_limit_bytes=SMALL_VMEM),
        name="local_terms",
    )(lists, pair_coupling, own_side, other_side, amps, fock_vv.reshape(vir_count, rows, width), fock_vv)

    received = lax.all_to_all(partial_sums.reshape(peers, rows, TILE), SAME_CORE, 0, 0, tiled=True)
    return pl.pallas_call(
        final_kernel,
        in_specs=[VMEM, VMEM, VMEM],
        out_specs=VMEM,
        out_shape=jax.ShapeDtypeStruct((rows, 1, width), F32),
        compiler_params=pltpu.CompilerParams(vmem_limit_bytes=SMALL_VMEM),
        name="final",
    )(received, local, tile_of_row)


def solution(mesh):
    grid = Mesh(mesh.devices.reshape(4, 2, 4, 4), ("z", "core", "x", "y"))
    pairs_of, rows_of = ("z", "core"), ("x", "y")
    in_specs = (P(rows_of, pairs_of, None), P(), P(pairs_of + rows_of, None, None), P(), P())
    out_specs = P(rows_of, pairs_of, None)
    return jax.shard_map(shards, mesh=grid, in_specs=in_specs, out_specs=out_specs, check_vma=False)
```

```python
import jax
import jax.numpy as jnp
from jax import lax
from jax.experimental import pallas as pl
from jax.experimental.pallas import tpu as pltpu
from jax.sharding import Mesh
from jax.sharding import PartitionSpec as P

F32 = jnp.float32
BF16 = jnp.bfloat16
NT = (((1,), (1,)), ((), ()))
TILE = 128
SAME_CORE = ("z", "x", "y")
LADDER_VMEM = 57 << 20
SMALL_VMEM = 8 << 20
COMPACT_VMEM = 57 << 20
AT_ONCE = 8


def place():
    vir = lax.axis_index("x") * lax.axis_size("y") + lax.axis_index("y")
    return lax.axis_index("z") * 2 + lax.axis_index("core"), vir


def row_tiles(vir, rows):
    first = vir * rows
    low = first // TILE
    high = (first + rows - 1) // TILE
    index = lax.broadcasted_iota(jnp.int32, (rows, TILE), 0) + first
    return low, high, index < (low + 1) * TILE


def compact_kernel(lists, amps, out):
    pair, vir = place()
    rows, width = amps.shape
    low, high, in_low = row_tiles(vir, rows)
    chosen = jnp.where(in_low, lists[low, 0, pair], lists[high, 0, pair])
    kept = jnp.zeros((rows, TILE), F32)
    for tile in range(width // TILE):
        part = amps[:, tile * TILE : (tile + 1) * TILE].astype(F32)
        kept = jnp.where(chosen == tile, part, kept)
    out[...] = jnp.broadcast_to(kept.astype(BF16)[None], out.shape)


def ladder_kernel(lists_in, amps, own, other, out, lists, factor, half, sums, sent, items, sems, list_sem, out_sems):
    core = lax.axis_index("core")
    pairs, tiles = amps.shape[0], lists.shape[0]
    depth = own.shape[0]
    width = tiles * TILE

    def copy(source, chunk, tile):
        b_rows = pl.ds(pl.multiple_of(tile * TILE, TILE), TILE)
        return pltpu.make_async_copy(source.at[:, b_rows, :], factor.at[chunk, :, b_rows, :], sems.at[chunk, tile])

    for tile in range(tiles):
        copy(own, 0, tile).start()
        if tile == 0:
            list_copy = pltpu.make_async_copy(lists_in, lists, list_sem)
            list_copy.start()
    list_copy.wait()
    count = jnp.int32(0)
    for tile in range(tiles):
        for pair in range(pairs):
            need = lists[0, 0, 2 * pair + core] == tile
            for row in range(1, tiles):
                need = need | (lists[row, 0, 2 * pair + core] == tile)
            items[count] = jnp.int32(pair * 8 + tile)
            count = count + need.astype(jnp.int32)

    def half_of(chunk, index):
        item = items[index]
        pair, tile = item // 8, item % 8
        b_rows = pl.ds(pl.multiple_of(tile * TILE, TILE), TILE)
        for tile_c in range(tiles):
            start = pl.multiple_of(lists[tile_c, 0, 2 * pair + core] * TILE, TILE)
            panel = factor[chunk, :, b_rows, pl.ds(start, TILE)].reshape(depth * TILE, TILE)
            rows = amps[pair, tile_c * TILE : (tile_c + 1) * TILE, :]
            result = lax.dot_general(rows, panel, NT, preferred_element_type=F32).astype(BF16)
            for level in range(depth):
                first = level * width + tile_c * TILE
                half[pair * tiles + tile, first : first + TILE, :] = result[:, level * TILE : (level + 1) * TILE]

    def wait_up_to(chunk, arrived, last):
        def one(tile, carry):
            copy(own, chunk, tile).wait()
            return carry

        lax.fori_loop(arrived, last + 1, one, 0)
        return jnp.maximum(arrived, last + 1)

    def one_chunk(chunk, carry):
        def several(first, size, arrived):
            arrived = wait_up_to(chunk, arrived, items[first + size - 1] % 8)
            for index in range(size):
                half_of(chunk, first + index)
            return arrived

        first, arrived, size = jnp.int32(0), jnp.int32(0), 1
        while size < AT_ONCE:
            odd = (count // size) % 2 == 1
            last = jnp.where(odd, items[jnp.minimum(first + size, count) - 1] % 8, -1)
            arrived = wait_up_to(chunk, arrived, last)

            @pl.when(odd)
            def _():
                for index in range(size):
                    half_of(chunk, first + index)

            first = jnp.where(odd, first + size, first)
            size *= 2
        arrived = lax.fori_loop(
            0, count // AT_ONCE, lambda step, seen: several(first + step * AT_ONCE, AT_ONCE, seen), arrived
        )
        wait_up_to(chunk, arrived, jnp.int32(tiles - 1))

        @pl.when(chunk == 0)
        def _():
            for tile in range(tiles):
                copy(other, 1, tile).start()

        @pl.when(chunk == 0)
        def _():
            for tile_a in range(tiles):
                for pair, (a_rows, value) in enumerate(products(0, tile_a)):
                    sums[pair, a_rows, :] = value

        return carry

    def products(chunk, tile_a):
        a_rows = pl.ds(tile_a * TILE, TILE)
        left = jnp.concatenate([factor[chunk, level, a_rows, :] for level in range(depth)], axis=1)
        right = jnp.concatenate(
            [half[pair * tiles + lists[tile_a, 0, 2 * pair + core]] for pair in range(pairs)], axis=1
        )
        result = jnp.dot(left, right, preferred_element_type=F32)
        return [(a_rows, result[:, pair * TILE : (pair + 1) * TILE]) for pair in range(pairs)]

    def send(tile):
        a_rows = pl.ds(tile * TILE, TILE)
        return pltpu.make_async_copy(sent.at[:, a_rows, :], out.at[:, a_rows, :], out_sems.at[tile])

    lax.fori_loop(0, 2, one_chunk, 0)
    for tile_a in range(tiles):
        for pair, (a_rows, value) in enumerate(products(1, tile_a)):
            sent[pair, a_rows, :] = (sums[pair, a_rows, :] + value).astype(BF16)
        send(tile_a).start()
    for tile_a in range(tiles):
        send(tile_a).wait()


def local_kernel(lists, coupling, own_side, other_side, amps, fock_rows, fock, out, tile_of_row):
    pair, vir = place()
    core = lax.axis_index("core")
    pairs, rows = own_side.shape[0], own_side.shape[1]
    tiles = lists.shape[0]
    low, high, in_low = row_tiles(vir, rows)
    tile_low, tile_high = lists[low, 0, pair], lists[high, 0, pair]
    total = jnp.zeros((rows, TILE), F32)
    for side, held in ((core, own_side), (1 - core, other_side)):
        for index in range(pairs):
            other = 2 * index + side
            weight = coupling[other, pair]
            none = jnp.float32(0)
            weight_low = jnp.where(lists[low, 0, other] == tile_low, weight, none)
            weight_high = jnp.where(lists[high, 0, other] == tile_high, weight, none)
            total = total + held[index].astype(F32) * jnp.where(in_low, weight_low, weight_high)
    chosen = jnp.where(in_low, tile_low, tile_high)
    masked = []
    for tile_c in range(tiles):
        part = fock_rows[vir, :, tile_c * TILE : (tile_c + 1) * TILE].astype(F32)
        masked.append(jnp.where(chosen == lists[tile_c, 0, pair], part, jnp.zeros_like(part)).astype(BF16))
    left = jnp.concatenate(masked, axis=1)
    total = total + jnp.dot(left, amps[pair // 2], preferred_element_type=F32)
    mine = own_side[pair // 2]
    for tile, keep in ((tile_low, in_low), (tile_high, jnp.logical_not(in_low))):
        span = pl.ds(pl.multiple_of(tile * TILE, TILE), TILE)
        product = lax.dot_general(mine, fock[span, span], NT, preferred_element_type=F32)
        total = total + jnp.where(keep, product, jnp.zeros_like(product))
    out[...] = total
    tile_of_row[...] = chosen


def final_kernel(sums, local, tile_of_row, out):
    chosen = tile_of_row[...]
    total = local[...] + jnp.sum(sums[...].astype(F32), axis=0)
    for tile in range(out.shape[2] // TILE):
        out[:, 0, tile * TILE : (tile + 1) * TILE] = jnp.where(chosen == tile, total, jnp.zeros_like(total))


SMEM = pl.BlockSpec(memory_space=pltpu.SMEM)
VMEM = pl.BlockSpec(memory_space=pltpu.VMEM)
ANY = pl.BlockSpec(memory_space=pl.ANY)


def in_hbm(array):
    return pltpu.with_memory_space_constraint(array, pltpu.HBM)


def in_vmem(array):
    return pltpu.with_memory_space_constraint(array, pltpu.VMEM)


def shards(amplitudes, tile_list, ladder_factor, fock_vv, pair_coupling):
    rows, _, width = amplitudes.shape
    depth = ladder_factor.shape[0]
    pairs = lax.axis_size("z")
    vir_count = lax.axis_size("x") * lax.axis_size("y")
    peers = pairs * vir_count
    swap = [(0, 1), (1, 0)]
    lists = jnp.transpose(tile_list, (1, 2, 0))
    tiles = lists.shape[0]
    _, vir = place()

    other_factor = lax.ppermute(ladder_factor, "core", swap)
    repeated = pl.pallas_call(
        compact_kernel,
        in_specs=[SMEM, VMEM],
        out_specs=VMEM,
        out_shape=pltpu.VMEM((peers, rows, TILE), BF16),
        compiler_params=pltpu.CompilerParams(vmem_limit_bytes=COMPACT_VMEM),
        name="compact",
    )(in_hbm(lists), in_hbm(amplitudes.reshape(rows, width)))
    gathered = lax.all_to_all(repeated, SAME_CORE, 0, 0, tiled=True)
    amps = gathered.reshape(pairs, width, TILE)

    partial_sums = pl.pallas_call(
        ladder_kernel,
        in_specs=[ANY, VMEM, ANY, ANY],
        out_specs=ANY,
        out_shape=jax.ShapeDtypeStruct((pairs, width, TILE), BF16),
        scratch_shapes=[
            pltpu.SMEM(lists.shape, jnp.int32),
            pltpu.VMEM((2, depth, width, width), BF16),
            pltpu.VMEM((pairs * tiles, depth * width, TILE), BF16),
            pltpu.VMEM((pairs, width, TILE), F32),
            pltpu.VMEM((pairs, width, TILE), BF16),
            pltpu.SMEM((pairs * tiles + 1,), jnp.int32),
            pltpu.SemaphoreType.DMA((2, tiles)),
            pltpu.SemaphoreType.DMA,
            pltpu.SemaphoreType.DMA((tiles,)),
        ],
        compiler_params=pltpu.CompilerParams(vmem_limit_bytes=LADDER_VMEM),
        cost_estimate=pl.CostEstimate(flops=17 * 10**9, bytes_accessed=20 * 10**6, transcendentals=0),
        name="ladder",
    )(in_hbm(lists), in_vmem(amps), in_hbm(ladder_factor), in_hbm(other_factor))

    own_side = lax.dynamic_index_in_dim(gathered.reshape(pairs, vir_count, rows, TILE), vir, 1, keepdims=False)
    other_side = lax.ppermute(own_side, "core", swap)
    local, tile_of_row = pl.pallas_call(
        local_kernel,
        in_specs=[SMEM, SMEM, VMEM, VMEM, VMEM, VMEM, VMEM],
        out_specs=(VMEM, VMEM),
        out_shape=(
            jax.ShapeDtypeStruct((rows, TILE), F32),
            jax.ShapeDtypeStruct((rows, TILE), jnp.int32),
        ),
        compiler_params=pltpu.CompilerParams(vmem_limit_bytes=SMALL_VMEM),
        name="local_terms",
    )(lists, pair_coupling, own_side, other_side, amps, fock_vv.reshape(vir_count, rows, width), fock_vv)

    received = lax.all_to_all(partial_sums.reshape(peers, rows, TILE), SAME_CORE, 0, 0, tiled=True)
    return pl.pallas_call(
        final_kernel,
        in_specs=[VMEM, VMEM, VMEM],
        out_specs=VMEM,
        out_shape=jax.ShapeDtypeStruct((rows, 1, width), F32),
        compiler_params=pltpu.CompilerParams(vmem_limit_bytes=SMALL_VMEM),
        name="final",
    )(received, local, tile_of_row)


def solution(mesh):
    grid = Mesh(mesh.devices.reshape(4, 2, 4, 4), ("z", "core", "x", "y"))
    pairs_of, rows_of = ("z", "core"), ("x", "y")
    in_specs = (P(rows_of, pairs_of, None), P(), P(pairs_of + rows_of, None, None), P(), P())
    out_specs = P(rows_of, pairs_of, None)
    return jax.shard_map(shards, mesh=grid, in_specs=in_specs, out_specs=out_specs, check_vma=False)
```

```python
import jax
import jax.numpy as jnp
from jax import lax
from jax.experimental import pallas as pl
from jax.experimental.pallas import tpu as pltpu
from jax.sharding import Mesh
from jax.sharding import PartitionSpec as P

F32 = jnp.float32
BF16 = jnp.bfloat16
NT = (((1,), (1,)), ((), ()))
TILE = 128
SAME_CORE = ("z", "x", "y")
LADDER_VMEM = 57 << 20
SMALL_VMEM = 8 << 20
COMPACT_VMEM = 57 << 20
AT_ONCE = 8


def place():
    vir = lax.axis_index("x") * lax.axis_size("y") + lax.axis_index("y")
    return lax.axis_index("z") * 2 + lax.axis_index("core"), vir


def row_tiles(vir, rows):
    first = vir * rows
    low = first // TILE
    high = (first + rows - 1) // TILE
    index = lax.broadcasted_iota(jnp.int32, (rows, TILE), 0) + first
    return low, high, index < (low + 1) * TILE


def compact_kernel(lists, amps, out):
    pair, vir = place()
    rows, width = amps.shape
    low, high, in_low = row_tiles(vir, rows)
    chosen = jnp.where(in_low, lists[low, 0, pair], lists[high, 0, pair])
    kept = jnp.zeros((rows, TILE), F32)
    for tile in range(width // TILE):
        part = amps[:, tile * TILE : (tile + 1) * TILE].astype(F32)
        kept = jnp.where(chosen == tile, part, kept)
    out[...] = jnp.broadcast_to(kept.astype(BF16)[None], out.shape)


def ladder_kernel(lists_in, amps, own, other, out, lists, factor, half, sums, sent, items, sems, list_sem, out_sems):
    core = lax.axis_index("core")
    pairs, tiles = amps.shape[0], lists.shape[0]
    depth = own.shape[0]
    width = tiles * TILE

    def copy(source, chunk, tile):
        b_rows = pl.ds(pl.multiple_of(tile * TILE, TILE), TILE)
        return pltpu.make_async_copy(source.at[:, b_rows, :], factor.at[chunk, :, b_rows, :], sems.at[chunk, tile])

    for tile in range(tiles):
        copy(own, 0, tile).start()
        if tile == 0:
            list_copy = pltpu.make_async_copy(lists_in, lists, list_sem)
            list_copy.start()
    list_copy.wait()
    for tile in range(tiles):
        copy(other, 1, tile).start()
    count = jnp.int32(0)
    for tile in range(tiles):
        for pair in range(pairs):
            need = lists[0, 0, 2 * pair + core] == tile
            for row in range(1, tiles):
                need = need | (lists[row, 0, 2 * pair + core] == tile)
            items[count] = jnp.int32(pair * 8 + tile)
            count = count + need.astype(jnp.int32)

    def half_of(chunk, index):
        item = items[index]
        pair, tile = item // 8, item % 8
        b_rows = pl.ds(pl.multiple_of(tile * TILE, TILE), TILE)
        for tile_c in range(tiles):
            start = pl.multiple_of(lists[tile_c, 0, 2 * pair + core] * TILE, TILE)
            panel = factor[chunk, :, b_rows, pl.ds(start, TILE)].reshape(depth * TILE, TILE)
            rows = amps[pair, tile_c * TILE : (tile_c + 1) * TILE, :]
            result = lax.dot_general(rows, panel, NT, preferred_element_type=F32).astype(BF16)
            for level in range(depth):
                first = level * width + tile_c * TILE
                half[pair * tiles + tile, first : first + TILE, :] = result[:, level * TILE : (level + 1) * TILE]

    def wait_up_to(chunk, arrived, last):
        def one(tile, carry):
            copy(own, chunk, tile).wait()
            return carry

        lax.fori_loop(arrived, last + 1, one, 0)
        return jnp.maximum(arrived, last + 1)

    def one_chunk(chunk, carry):
        def several(first, size, arrived):
            arrived = wait_up_to(chunk, arrived, items[first + size - 1] % 8)
            for index in range(size):
                half_of(chunk, first + index)
            return arrived

        first, arrived, size = jnp.int32(0), jnp.int32(0), 1
        while size < AT_ONCE:
            odd = (count // size) % 2 == 1
            last = jnp.where(odd, items[jnp.minimum(first + size, count) - 1] % 8, -1)
            arrived = wait_up_to(chunk, arrived, last)

            @pl.when(odd)
            def _():
                for index in range(size):
                    half_of(chunk, first + index)

            first = jnp.where(odd, first + size, first)
            size *= 2
        arrived = lax.fori_loop(
            0, count // AT_ONCE, lambda step, seen: several(first + step * AT_ONCE, AT_ONCE, seen), arrived
        )
        wait_up_to(chunk, arrived, jnp.int32(tiles - 1))

        @pl.when(chunk == 0)
        def _():
            for tile_a in range(tiles):
                for pair, (a_rows, value) in enumerate(products(0, tile_a)):
                    sums[pair, a_rows, :] = value

        return carry

    def products(chunk, tile_a):
        a_rows = pl.ds(tile_a * TILE, TILE)
        left = jnp.concatenate([factor[chunk, level, a_rows, :] for level in range(depth)], axis=1)
        right = jnp.concatenate(
            [half[pair * tiles + lists[tile_a, 0, 2 * pair + core]] for pair in range(pairs)], axis=1
        )
        result = jnp.dot(left, right, preferred_element_type=F32)
        return [(a_rows, result[:, pair * TILE : (pair + 1) * TILE]) for pair in range(pairs)]

    def send(tile):
        a_rows = pl.ds(tile * TILE, TILE)
        return pltpu.make_async_copy(sent.at[:, a_rows, :], out.at[:, a_rows, :], out_sems.at[tile])

    lax.fori_loop(0, 2, one_chunk, 0)
    for tile_a in range(tiles):
        for pair, (a_rows, value) in enumerate(products(1, tile_a)):
            sent[pair, a_rows, :] = (sums[pair, a_rows, :] + value).astype(BF16)
        send(tile_a).start()
    for tile_a in range(tiles):
        send(tile_a).wait()


def local_kernel(lists, coupling, own_side, other_side, amps, fock_rows, fock, out, tile_of_row):
    pair, vir = place()
    core = lax.axis_index("core")
    pairs, rows = own_side.shape[0], own_side.shape[1]
    tiles = lists.shape[0]
    low, high, in_low = row_tiles(vir, rows)
    tile_low, tile_high = lists[low, 0, pair], lists[high, 0, pair]
    total = jnp.zeros((rows, TILE), F32)
    for side, held in ((core, own_side), (1 - core, other_side)):
        for index in range(pairs):
            other = 2 * index + side
            weight = coupling[other, pair]
            none = jnp.float32(0)
            weight_low = jnp.where(lists[low, 0, other] == tile_low, weight, none)
            weight_high = jnp.where(lists[high, 0, other] == tile_high, weight, none)
            total = total + held[index].astype(F32) * jnp.where(in_low, weight_low, weight_high)
    chosen = jnp.where(in_low, tile_low, tile_high)
    masked = []
    for tile_c in range(tiles):
        part = fock_rows[vir, :, tile_c * TILE : (tile_c + 1) * TILE].astype(F32)
        masked.append(jnp.where(chosen == lists[tile_c, 0, pair], part, jnp.zeros_like(part)).astype(BF16))
    left = jnp.concatenate(masked, axis=1)
    total = total + jnp.dot(left, amps[pair // 2], preferred_element_type=F32)
    mine = own_side[pair // 2]
    for tile, keep in ((tile_low, in_low), (tile_high, jnp.logical_not(in_low))):
        span = pl.ds(pl.multiple_of(tile * TILE, TILE), TILE)
        product = lax.dot_general(mine, fock[span, span], NT, preferred_element_type=F32)
        total = total + jnp.where(keep, product, jnp.zeros_like(product))
    out[...] = total
    tile_of_row[...] = chosen


def final_kernel(sums, local, tile_of_row, out):
    chosen = tile_of_row[...]
    total = local[...] + jnp.sum(sums[...].astype(F32), axis=0)
    for tile in range(out.shape[2] // TILE):
        out[:, 0, tile * TILE : (tile + 1) * TILE] = jnp.where(chosen == tile, total, jnp.zeros_like(total))


SMEM = pl.BlockSpec(memory_space=pltpu.SMEM)
VMEM = pl.BlockSpec(memory_space=pltpu.VMEM)
ANY = pl.BlockSpec(memory_space=pl.ANY)


def in_hbm(array):
    return pltpu.with_memory_space_constraint(array, pltpu.HBM)


def in_vmem(array):
    return pltpu.with_memory_space_constraint(array, pltpu.VMEM)


def shards(amplitudes, tile_list, ladder_factor, fock_vv, pair_coupling):
    rows, _, width = amplitudes.shape
    depth = ladder_factor.shape[0]
    pairs = lax.axis_size("z")
    vir_count = lax.axis_size("x") * lax.axis_size("y")
    peers = pairs * vir_count
    swap = [(0, 1), (1, 0)]
    lists = jnp.transpose(tile_list, (1, 2, 0))
    tiles = lists.shape[0]
    _, vir = place()

    other_factor = lax.ppermute(ladder_factor, "core", swap)
    repeated = pl.pallas_call(
        compact_kernel,
        in_specs=[SMEM, VMEM],
        out_specs=VMEM,
        out_shape=pltpu.VMEM((peers, rows, TILE), BF16),
        compiler_params=pltpu.CompilerParams(vmem_limit_bytes=COMPACT_VMEM),
        name="compact",
    )(in_hbm(lists), in_hbm(amplitudes.reshape(rows, width)))
    gathered = lax.all_to_all(repeated, SAME_CORE, 0, 0, tiled=True)
    amps = gathered.reshape(pairs, width, TILE)

    partial_sums = pl.pallas_call(
        ladder_kernel,
        in_specs=[ANY, VMEM, ANY, ANY],
        out_specs=ANY,
        out_shape=jax.ShapeDtypeStruct((pairs, width, TILE), BF16),
        scratch_shapes=[
            pltpu.SMEM(lists.shape, jnp.int32),
            pltpu.VMEM((2, depth, width, width), BF16),
            pltpu.VMEM((pairs * tiles, depth * width, TILE), BF16),
            pltpu.VMEM((pairs, width, TILE), F32),
            pltpu.VMEM((pairs, width, TILE), BF16),
            pltpu.SMEM((pairs * tiles + 1,), jnp.int32),
            pltpu.SemaphoreType.DMA((2, tiles)),
            pltpu.SemaphoreType.DMA,
            pltpu.SemaphoreType.DMA((tiles,)),
        ],
        compiler_params=pltpu.CompilerParams(vmem_limit_bytes=LADDER_VMEM),
        cost_estimate=pl.CostEstimate(flops=17 * 10**9, bytes_accessed=20 * 10**6, transcendentals=0),
        name="ladder",
    )(in_hbm(lists), in_vmem(amps), in_hbm(ladder_factor), in_hbm(other_factor))

    own_side = lax.dynamic_index_in_dim(gathered.reshape(pairs, vir_count, rows, TILE), vir, 1, keepdims=False)
    other_side = lax.ppermute(own_side, "core", swap)
    local, tile_of_row = pl.pallas_call(
        local_kernel,
        in_specs=[SMEM, SMEM, VMEM, VMEM, VMEM, VMEM, VMEM],
        out_specs=(VMEM, VMEM),
        out_shape=(
            jax.ShapeDtypeStruct((rows, TILE), F32),
            jax.ShapeDtypeStruct((rows, TILE), jnp.int32),
        ),
        compiler_params=pltpu.CompilerParams(vmem_limit_bytes=SMALL_VMEM),
        name="local_terms",
    )(lists, pair_coupling, own_side, other_side, amps, fock_vv.reshape(vir_count, rows, width), fock_vv)

    received = lax.all_to_all(partial_sums.reshape(peers, rows, TILE), SAME_CORE, 0, 0, tiled=True)
    return pl.pallas_call(
        final_kernel,
        in_specs=[VMEM, VMEM, VMEM],
        out_specs=VMEM,
        out_shape=jax.ShapeDtypeStruct((rows, 1, width), F32),
        compiler_params=pltpu.CompilerParams(vmem_limit_bytes=SMALL_VMEM),
        name="final",
    )(received, local, tile_of_row)


def solution(mesh):
    grid = Mesh(mesh.devices.reshape(4, 2, 4, 4), ("z", "core", "x", "y"))
    pairs_of, rows_of = ("z", "core"), ("x", "y")
    in_specs = (P(rows_of, pairs_of, None), P(), P(pairs_of + rows_of, None, None), P(), P())
    out_specs = P(rows_of, pairs_of, None)
    return jax.shard_map(shards, mesh=grid, in_specs=in_specs, out_specs=out_specs, check_vma=False)
```
